256 devices in a mesh: dp: 16 (over y, x), ctx: 16 (over z, core).
Axes of the slice: x: 4, y: 4, z: 8, core: 2. Of those that a mesh axis runs over, the one named last changes fastest.
Arguments:
- queries: bfloat16 [65536, 512], P(('dp', 'ctx')), parts along dimension 0, may hold values from -32 to 32
- keys: bfloat16 [65536, 128], P(('dp', 'ctx')), parts along dimension 0, may hold values from -6 to 6
- values: bfloat16 [65536, 128], P(('dp', 'ctx')), parts along dimension 0, may hold values from -6 to 6
- out_grad: bfloat16 [65536, 512], P(('dp', 'ctx')), parts along dimension 0, may hold values from -6 to 6
- span_order: int32 [512], P('dp'), parts along dimension 0, may hold values from 0 to 31, each once
Outputs:
- query_grad: bfloat16 [65536, 512], P(('dp', 'ctx')), parts along dimension 0
- key_grad: bfloat16 [65536, 128], P(('dp', 'ctx')), parts along dimension 0
- value_grad: bfloat16 [65536, 128], P(('dp', 'ctx')), parts along dimension 0
The draws below stay inside these ranges and needn't reach their ends.
There are 16 independent parts, one for each index of `dp`. The reference program is written for one: setup_inputs(seed, part) draws one part's arguments, and reference() takes and returns one part's arrays. A program takes and returns all parts, laid end to end along the dimension named above; each array names one. Nothing has to cross between parts.
All inputs are finite; a program needn't handle non-finite values.
Results may differ from the reference program's by a relative error of at most 0.02.
Values may be sent and summed in bfloat16 or wider, within the bound.
A program may use at most 128 MiB of HBM per device.

```python
import jax
import jax.numpy as jnp

HD = 128
HEADS = 4
HALF = 128
SPANS = 32
SEQ = 4096


def draw_keys(key, part):
    base = jnp.clip(jax.random.normal(jax.random.fold_in(key, 1), (SEQ, HD), jnp.float32), -6.0, 6.0)
    result = base
    return result.astype(jnp.bfloat16)


def draw_queries(key, part):
    base = jnp.clip(jax.random.normal(jax.random.fold_in(key, 4), (SEQ, HEADS * HD), jnp.float32), -6.0, 6.0)
    result = base
    return result.astype(jnp.bfloat16)


def block_scale(rng, extent, shards, low, largest):
    def one(dim, parts):
        draws = jax.random.uniform(jax.random.fold_in(jax.random.fold_in(rng, 6), dim), (parts,), jnp.float32, low / len(shards), largest / len(shards))
        return jnp.repeat(jnp.exp(draws), extent[dim] // parts).reshape((-1,) + (1,) * (len(extent) - dim - 1))

    gain = one(*shards[0])
    for cut in shards[1:]:
        gain = gain * one(*cut)
    return gain


def gaussian(own_key, extent, deviation, reach, split=(), held_as=jnp.bfloat16):
    values = deviation * jax.random.normal(own_key, extent, jnp.float32)
    if split:
        values = values * block_scale(own_key, extent, split, -0.22, 0.18)
    return jnp.clip(values, -reach, reach).astype(held_as)


def setup_inputs(seed: int = 0, part: int = 0) -> dict:
    streams_of = jax.random.split(jax.random.key(seed), 6)
    part_splits = jax.random.split(jax.random.fold_in(streams_of[5], part), 6)
    queries = draw_queries(jax.random.fold_in(jax.random.fold_in(streams_of[5], part), 71), part)
    keys = draw_keys(jax.random.fold_in(jax.random.fold_in(streams_of[5], part), 71), part)
    values = gaussian(part_splits[2], (SEQ, HD), 1.0, 6.0, ((0, 16),))
    out_grad = gaussian(part_splits[3], (SEQ, HEADS * HD), 1.0, 6.0, ((0, 16),))
    span_order = jax.random.permutation(part_splits[4], SPANS).astype(jnp.int32)
    return {"queries": queries, "keys": keys, "values": values, "out_grad": out_grad, "span_order": span_order}


def reference(queries, keys, values, out_grad, span_order):
    softmax_scale = HD ** -0.5
    position = (span_order[:, None] * HALF + jnp.arange(HALF, dtype=jnp.int32)[None, :]).reshape(-1)
    visible = position[None, :] <= position[:, None]
    key_total = jnp.zeros((SEQ, HD), jnp.float32)
    value_total = jnp.zeros((SEQ, HD), jnp.float32)
    query_parts = []
    for head in range(HEADS):
        query_head = queries[:, head * HD:(head + 1) * HD]
        grad_head = out_grad[:, head * HD:(head + 1) * HD]
        scores = jnp.dot(query_head, keys.T, preferred_element_type=jnp.float32) * softmax_scale
        masked = jnp.where(visible, scores, -jnp.inf)
        row_max = jnp.max(masked, axis=1)
        log_total = row_max + jnp.log(jnp.sum(jnp.exp(masked - row_max[:, None]), axis=1))
        prob = jnp.where(visible, jnp.exp(scores - log_total[:, None]), 0.0)
        prob_grad = jnp.dot(grad_head, values.T, preferred_element_type=jnp.float32)
        delta = jnp.sum(prob * prob_grad, axis=1)
        prob_low = prob.astype(jnp.bfloat16)
        score_grad = (prob * (prob_grad - delta[:, None]) * softmax_scale).astype(jnp.bfloat16)
        query_parts.append(jnp.dot(score_grad, keys, preferred_element_type=jnp.float32).astype(jnp.bfloat16))
        key_total = key_total + jnp.dot(score_grad.T, query_head, preferred_element_type=jnp.float32)
        value_total = value_total + jnp.dot(prob_low.T, grad_head, preferred_element_type=jnp.float32)
    query_grad = jnp.concatenate(query_parts, axis=1)
    return query_grad, key_total.astype(jnp.bfloat16), value_total.astype(jnp.bfloat16)
```

```python
import functools
import math

import jax
import jax.numpy as jnp
from jax import lax
from jax.experimental import pallas as pl
from jax.experimental.pallas import tpu as pltpu
from jax.sharding import PartitionSpec as P

MESH = pl.DeviceIdType.MESH
F32 = jnp.float32
BF16 = jnp.bfloat16
HIDDEN = -1e30
UP, DOWN = 0, 1
KEY, VALUE = 0, 1


def block_positions(order_ref, device, rows, half_rows, shape, dim):
    index = lax.broadcasted_iota(jnp.int32, shape, dim)
    blocks = rows // half_rows
    position = None
    for b in range(blocks):
        here = order_ref[device * blocks + b] * half_rows + (index - b * half_rows)
        position = here if position is None else jnp.where(index >= b * half_rows, here, position)
    return position


def kernel(
    chips, heads, unroll,
    q_in, k_in, v_in, g_in, order_ref,
    dq_out, dk_out, dv_out,
    q_raw, g_raw, q_rows, g_rows, q_cols, g_cols,
    k_all, v_all, k_cols, e_all, p_all, m_all, l_all, d_all,
    stat_out, stat_in, factor, delta, query_pos,
    term, dq_cols, dq_recv, ring_out, ring_in, dq_stage, dk_stage, dv_stage,
    local_sem, pair_send, pair_recv, gather_send, gather_recv, ring_send, ring_recv,
):
    rows, head_size = k_in.shape
    half_rows = chips * 2 * rows // order_ref.shape[0]
    tiles = 2 * heads
    far = chips // 2
    softmax_scale = head_size ** (-0.5)
    exponent_scale = softmax_scale * math.log2(math.e)

    me = lax.axis_index("ctx")
    chip, core = me // 2, me % 2
    partner = chip * 2 + (1 - core)

    def at_chip(offset):
        return lax.rem(chip + (offset + chips), chips) * 2 + core

    above, below = at_chip(1), at_chip(-1)

    barrier = pltpu.get_barrier_semaphore()
    for other in (above, below, partner):
        pl.semaphore_signal(barrier, inc=1, device_id={"ctx": other}, device_id_type=MESH)

    own = [
        pltpu.make_async_copy(src, dst, local_sem.at[i])
        for i, (src, dst) in enumerate(
            ((k_in, k_all.at[0]), (v_in, v_all.at[0]), (q_in, q_raw.at[0]), (g_in, g_raw.at[0]))
        )
    ]
    for copy in own:
        copy.start()

    def slot(way, distance):
        return (chips - distance) % chips if way == UP else distance

    def gather_copy(way, distance, part):
        source = (k_in, v_in)[part] if distance == 1 else (k_all, v_all)[part].at[slot(way, distance - 1)]
        return pltpu.make_async_remote_copy(
            src_ref=source,
            dst_ref=(k_all, v_all)[part].at[slot(way, distance)],
            send_sem=gather_send.at[way, distance - 1, part],
            recv_sem=gather_recv.at[way, distance - 1, part],
            device_id={"ctx": above if way == UP else below},
            device_id_type=MESH,
        )

    def travels(way, distance, part):
        return distance < far or (distance == far and (way == UP) == (part == KEY))

    def pair_copy(index, source, target):
        return pltpu.make_async_remote_copy(
            src_ref=source,
            dst_ref=target,
            send_sem=pair_send.at[index],
            recv_sem=pair_recv.at[index],
            device_id={"ctx": partner},
            device_id_type=MESH,
        )

    def ring_copy(way, distance, part):
        return pltpu.make_async_remote_copy(
            src_ref=ring_out.at[way, distance - 1, part],
            dst_ref=ring_in.at[way, distance - 1, part],
            send_sem=ring_send.at[way, distance - 1, part],
            recv_sem=ring_recv.at[way, distance - 1, part],
            device_id={"ctx": above if way == UP else below},
            device_id_type=MESH,
        )

    started = []

    def start(copy):
        copy.start()
        started.append(copy)

    pl.semaphore_wait(barrier, 3)

    for part in (KEY, VALUE):
        for way in (UP, DOWN):
            start(gather_copy(way, 1, part))
    pair_q = pair_copy(0, q_in, q_raw.at[1])
    pair_g = pair_copy(1, g_in, g_raw.at[1])
    start(pair_q)
    start(pair_g)

    def spread(half):
        for h in range(heads):
            columns = slice(h * head_size, (h + 1) * head_size)
            for raw, by_row, by_col in ((q_raw, q_rows, q_cols), (g_raw, g_rows, g_cols)):
                tile = raw[half, :, columns]
                by_row[half * heads + h] = tile
                by_col[half * heads + h] = tile.T
        query_pos[half] = block_positions(order_ref, me if half == 0 else partner, rows, half_rows, (8, rows), 1)

    def pass_one(where, device):
        k_cols[where] = k_all[where].T
        key_pos = block_positions(order_ref, device, rows, half_rows, (rows, rows), 0)

        def one(t):
            keys = k_all[where]
            scores = jnp.dot(keys, q_cols[t], preferred_element_type=F32)
            visible = key_pos <= query_pos[t // heads, 0:1, :]
            scores = jnp.where(visible, scores, HIDDEN)
            top = jnp.max(scores, axis=0, keepdims=True)
            e = jnp.exp2((scores - top) * exponent_scale)
            prob_grad = jnp.dot(v_all[where], g_cols[t], preferred_element_type=F32)
            e_all[where, t] = e
            p_all[where, t] = prob_grad
            m_all[t, where : where + 1, :] = top
            l_all[t, where : where + 1, :] = jnp.sum(e, axis=0, keepdims=True)
            d_all[t, where : where + 1, :] = jnp.sum(e * prob_grad, axis=0, keepdims=True)

        def body(i, carry):
            for u in range(unroll):
                one(i * unroll + u)
            return carry

        lax.fori_loop(0, tiles // unroll, body, 0)

    for copy in own:
        copy.wait()
    spread(0)
    pair_q.wait_recv()
    pair_g.wait_recv()
    spread(1)

    def relay(distance, part):
        for way in (UP, DOWN):
            if travels(way, distance, part):
                gather_copy(way, distance, part).wait_recv()
                if distance < far and travels(way, distance + 1, part):
                    start(gather_copy(way, distance + 1, part))

    relay(1, KEY)
    pass_one(0, me)
    relay(1, VALUE)
    for distance in range(1, far + 1):
        if distance > 1:
            relay(distance, KEY)
            relay(distance, VALUE)
        if distance < far:
            pass_one(slot(UP, distance), at_chip(-distance))
        pass_one(slot(DOWN, distance), at_chip(distance))

    stat_out[...] = jnp.zeros_like(stat_out)
    for t in range(tiles):
        top = jnp.max(m_all[t], axis=0, keepdims=True)
        weight = jnp.exp2((m_all[t] - top) * exponent_scale)
        stat_out[t, 0:1, :] = top
        stat_out[t, 1:2, :] = jnp.sum(l_all[t] * weight, axis=0, keepdims=True)
        stat_out[t, 2:3, :] = jnp.sum(d_all[t] * weight, axis=0, keepdims=True)
        factor[t] = weight
    stat_copies = []
    for i in range(2):
        copy = pair_copy(
            2 + i,
            stat_out.at[pl.ds(i * heads, heads)],
            stat_in.at[pl.ds((1 - i) * heads, heads)],
        )
        start(copy)
        stat_copies.append(copy)
    for copy in stat_copies:
        copy.wait_recv()
    for t in range(tiles):
        top_here, top_there = stat_out[t, 0:1, :], stat_in[t, 0:1, :]
        top = jnp.maximum(top_here, top_there)
        here = jnp.exp2((top_here - top) * exponent_scale)
        there = jnp.exp2((top_there - top) * exponent_scale)
        inverse = 1.0 / (stat_out[t, 1:2, :] * here + stat_in[t, 1:2, :] * there)
        delta[t] = jnp.broadcast_to(
            (stat_out[t, 2:3, :] * here + stat_in[t, 2:3, :] * there) * inverse, delta.shape[1:]
        )
        factor[t] = factor[t] * (here * inverse)

    dq_cols[...] = jnp.zeros_like(dq_cols)
    term[...] = jnp.zeros_like(term)

    def pass_two(where):
        def one(t):
            prob = e_all[where, t] * factor[t, where : where + 1, :]
            score_grad = (prob * (p_all[where, t] - delta[t, 0:1, :])).astype(BF16)
            term[where, VALUE] += jnp.dot(prob.astype(BF16), g_rows[t], preferred_element_type=F32)
            term[where, KEY] += jnp.dot(score_grad, q_rows[t], preferred_element_type=F32)
            dq_cols[t] += jnp.dot(k_cols[where], score_grad, preferred_element_type=F32)

        def body(i, carry):
            for u in range(unroll):
                one(i * unroll + u)
            return carry

        lax.fori_loop(0, tiles // unroll, body, 0)

    def own_term(where, part):
        value = term[where, part]
        return value * softmax_scale if part == KEY else value

    def ring_step(way, distance, part):
        if not travels(way, distance, part):
            return
        value = own_term(slot(1 - way, distance), part)
        if distance < far and travels(way, distance + 1, part):
            ring_copy(way, distance + 1, part).wait_recv()
            value = value + ring_in[way, distance, part].astype(F32)
        ring_out[way, distance - 1, part] = value.astype(BF16)
        start(ring_copy(way, distance, part))

    pass_two(far)
    ring_step(UP, far, KEY)
    ring_step(DOWN, far, VALUE)
    for distance in range(far - 1, 0, -1):
        for way in (UP, DOWN):
            pass_two(slot(1 - way, distance))
            if distance == far - 1:
                ring_step(way, distance, VALUE if way == UP else KEY)
        if distance == 1:
            pass_two(0)
            pair_dq = pair_copy(4, dq_cols.at[pl.ds(heads, heads)], dq_recv)
            start(pair_dq)
        if distance == far - 1:
            ring_step(UP, distance, KEY)
            ring_step(DOWN, distance, VALUE)
        else:
            for part in (KEY, VALUE):
                for way in (UP, DOWN):
                    ring_step(way, distance, part)

    pair_dq.wait_recv()
    for h in range(heads):
        total = (dq_cols[h] + dq_recv[h]) * softmax_scale
        dq_stage[:, h * head_size : (h + 1) * head_size] = total.T.astype(BF16)
    out = [pltpu.make_async_copy(dq_stage, dq_out, local_sem.at[4])]
    out[0].start()
    for part, stage, target in ((KEY, dk_stage, dk_out), (VALUE, dv_stage, dv_out)):
        value = own_term(0, part)
        for way in (UP, DOWN):
            ring_copy(way, 1, part).wait_recv()
            value = value + ring_in[way, 0, part].astype(F32)
        stage[...] = value.astype(BF16)
        copy = pltpu.make_async_copy(stage, target, local_sem.at[5 + part])
        copy.start()
        out.append(copy)
    for copy in started:
        copy.wait_send()
    for copy in out:
        copy.wait()


def solution(mesh):
    devices = mesh.shape["ctx"]
    chips = devices // 2
    far = chips // 2

    def on_device(queries, keys, values, out_grad, span_order):
        rows, head_size = keys.shape
        heads = queries.shape[1] // head_size
        tiles = 2 * heads
        any_spec = pl.BlockSpec(memory_space=pl.ANY)
        vmem = pltpu.VMEM
        elements = chips * tiles * rows * rows
        return pl.pallas_call(
            functools.partial(kernel, chips, heads, 2),
            name="ring_attention_backward",
            out_shape=(
                jax.ShapeDtypeStruct(queries.shape, BF16),
                jax.ShapeDtypeStruct(keys.shape, BF16),
                jax.ShapeDtypeStruct(values.shape, BF16),
            ),
            in_specs=[any_spec] * 4 + [pl.BlockSpec(memory_space=pltpu.SMEM)],
            out_specs=(any_spec,) * 3,
            scratch_shapes=[
                vmem((2, rows, heads * head_size), BF16),
                vmem((2, rows, heads * head_size), BF16),
                vmem((tiles, rows, head_size), BF16),
                vmem((tiles, rows, head_size), BF16),
                vmem((tiles, head_size, rows), BF16),
                vmem((tiles, head_size, rows), BF16),
                vmem((chips, rows, head_size), BF16),
                vmem((chips, rows, head_size), BF16),
                vmem((chips, head_size, rows), BF16),
                vmem((chips, tiles, rows, rows), F32),
                vmem((chips, tiles, rows, rows), F32),
                vmem((tiles, chips, rows), F32),
                vmem((tiles, chips, rows), F32),
                vmem((tiles, chips, rows), F32),
                vmem((tiles, 8, rows), F32),
                vmem((tiles, 8, rows), F32),
                vmem((tiles, chips, rows), F32),
                vmem((tiles, 8, rows), F32),
                vmem((2, 8, rows), jnp.int32),
                vmem((chips, 2, rows, head_size), F32),
                vmem((tiles, head_size, rows), F32),
                vmem((heads, head_size, rows), F32),
                vmem((2, far, 2, rows, head_size), BF16),
                vmem((2, far, 2, rows, head_size), BF16),
                vmem((rows, heads * head_size), BF16),
                vmem((rows, head_size), BF16),
                vmem((rows, head_size), BF16),
                pltpu.SemaphoreType.DMA((7,)),
                pltpu.SemaphoreType.DMA((5,)),
                pltpu.SemaphoreType.DMA((5,)),
                pltpu.SemaphoreType.DMA((2, far, 2)),
                pltpu.SemaphoreType.DMA((2, far, 2)),
                pltpu.SemaphoreType.DMA((2, far, 2)),
                pltpu.SemaphoreType.DMA((2, far, 2)),
            ],
            compiler_params=pltpu.CompilerParams(
                collective_id=0,
                has_side_effects=True,
                vmem_limit_bytes=58 * 1024 * 1024,
            ),
            cost_estimate=pl.CostEstimate(
                flops=10 * elements * head_size,
                bytes_accessed=2 * (2 * queries.size * 2 + 3 * keys.size * 2),
                transcendentals=elements,
            ),
        )(queries, keys, values, out_grad, span_order)

    row = P(("dp", "ctx"), None)
    return jax.shard_map(
        on_device,
        mesh=mesh,
        in_specs=(row, row, row, row, P("dp")),
        out_specs=(row, row, row),
        check_vma=False,
    )
```

```python
import functools
import math

import jax
import jax.numpy as jnp
from jax import lax
from jax.experimental import pallas as pl
from jax.experimental.pallas import tpu as pltpu
from jax.sharding import PartitionSpec as P

MESH = pl.DeviceIdType.MESH
F32 = jnp.float32
BF16 = jnp.bfloat16
HIDDEN = -1e30
UP, DOWN = 0, 1
KEY, VALUE = 0, 1


def block_of_row(order_ref, device, blocks, half_rows, shape):
    index = lax.broadcasted_iota(jnp.int32, shape, len(shape) - 1)
    result = jnp.full(shape, order_ref[device * blocks], jnp.int32)
    for b in range(1, blocks):
        result = jnp.where(index >= b * half_rows, order_ref[device * blocks + b], result)
    return result


def kernel(
    chips, heads,
    q_in, k_in, v_in, g_in, order_in,
    dq_out, dk_out, dv_out,
    q_raw, g_raw, q_cols, g_cols,
    k_all, v_all, k_cols, e_all, p_all, m_all, l_all, d_all,
    stat_out, stat_in, factor, delta, query_block, key_block,
    term, dq_cols, dq_recv, ring_out, ring_in, dq_stage, dk_stage, dv_stage,
    order_ref, local_sem, pair_send, pair_recv, sent, gather_recv, ring_recv,
):
    rows, head_size = k_in.shape
    half_rows = chips * 2 * rows // order_in.shape[0]
    blocks = rows // half_rows
    tiles = 2 * heads
    far = chips // 2
    softmax_scale = head_size ** (-0.5)
    exponent_scale = softmax_scale * math.log2(math.e)

    me = lax.axis_index("ctx")
    chip, core = me // 2, me % 2
    partner = chip * 2 + (1 - core)

    def at_chip(offset):
        return lax.rem(chip + (offset + chips), chips) * 2 + core

    above, below = at_chip(1), at_chip(-1)

    barrier = pltpu.get_barrier_semaphore()
    for other in (above, below, partner):
        pl.semaphore_signal(barrier, inc=1, device_id={"ctx": other}, device_id_type=MESH)

    own = [
        pltpu.make_async_copy(src, dst, local_sem.at[i])
        for i, (src, dst) in enumerate(
            ((q_in, q_raw.at[0]), (g_in, g_raw.at[0]), (k_in, k_all.at[0]), (v_in, v_all.at[0]), (order_in, order_ref))
        )
    ]
    for copy in own:
        copy.start()

    def slot(way, distance):
        return (chips - distance) % chips if way == UP else distance

    def head_columns(h):
        return slice(h * head_size, (h + 1) * head_size)

    def part_rows(b):
        return slice(b * half_rows, (b + 1) * half_rows)

    def gather_copy(way, distance, part, b):
        here = pl.ds(b * half_rows, half_rows)
        all_rows = (k_all, v_all)[part]
        return pltpu.make_async_remote_copy(
            src_ref=(k_in, v_in)[part].at[here] if distance == 1 else all_rows.at[slot(way, distance - 1), here],
            dst_ref=all_rows.at[slot(way, distance), here],
            send_sem=sent.at[0],
            recv_sem=gather_recv.at[way, distance - 1, part, b],
            device_id={"ctx": above if way == UP else below},
            device_id_type=MESH,
        )

    def travels(way, distance, b):
        return distance < far or (distance == far and (way == UP) == (b < blocks // 2))

    def pair_copy(index, source, target):
        return pltpu.make_async_remote_copy(
            src_ref=source,
            dst_ref=target,
            send_sem=pair_send.at[index],
            recv_sem=pair_recv.at[index],
            device_id={"ctx": partner},
            device_id_type=MESH,
        )

    def ring_copy(way, distance, part, b):
        return pltpu.make_async_remote_copy(
            src_ref=ring_out.at[way, distance - 1, part, b],
            dst_ref=ring_in.at[way, distance - 1, part, b],
            send_sem=sent.at[0],
            recv_sem=ring_recv.at[way, distance - 1, part, b],
            device_id={"ctx": above if way == UP else below},
            device_id_type=MESH,
        )

    started = []
    sends = []

    def start(copy, sends=started):
        copy.start()
        sends.append(copy)

    pl.semaphore_wait(barrier, 3)

    for part in (KEY, VALUE):
        for b in range(blocks):
            for way in (UP, DOWN):
                if travels(way, 1, b):
                    start(gather_copy(way, 1, part, b), sends)
    pair_q = pair_copy(0, q_in, q_raw.at[1])
    pair_g = pair_copy(1, g_in, g_raw.at[1])
    start(pair_q)
    start(pair_g)
    dq_cols[...] = jnp.zeros_like(dq_cols)
    stat_out[...] = jnp.zeros_like(stat_out)

    def spread(half):
        for h in range(heads):
            columns = head_columns(h)
            q_cols[half * heads + h] = q_raw[half, :, columns].T
            g_cols[half * heads + h] = g_raw[half, :, columns].T
        query_block[half] = block_of_row(order_ref, me if half == 0 else partner, blocks, half_rows, (8, rows))

    once = (me + 2 * chips) // (2 * chips)

    def over_tiles(body):
        def step(i, carry):
            body(range(tiles))
            return carry

        lax.fori_loop(0, once, step, 0)

    def pass_one(where, device, diagonal=False):
        k_cols[where] = k_all[where].T
        for b in range(blocks):
            key_block[where * blocks + b : where * blocks + b + 1, :] = jnp.full(
                (1, rows), order_ref[device * blocks + b], jnp.int32
            )

        def one(t):
            scores = jnp.dot(k_all[where], q_cols[t], preferred_element_type=F32)
            prob_grad = jnp.dot(v_all[where], g_cols[t], preferred_element_type=F32)
            p_all[where, t] = prob_grad
            for b in range(blocks):
                r = where * blocks + b
                block = scores[part_rows(b)]
                if diagonal and t < heads:
                    key_row = lax.broadcasted_iota(jnp.int32, block.shape, 0) + b * half_rows
                    query_row = lax.broadcasted_iota(jnp.int32, block.shape, 1)
                    limit = jnp.where(query_row < (b + 1) * half_rows, query_row, rows)
                    limit = jnp.where(query_row < b * half_rows, rows, limit)
                    block = jnp.where(key_row > limit, HIDDEN, block)
                top = jnp.max(block, axis=0, keepdims=True)
                e = jnp.exp2((block - top) * exponent_scale)
                e_all[where, t, part_rows(b)] = e
                m_all[t, r : r + 1, :] = top
                l_all[t, r : r + 1, :] = jnp.sum(e, axis=0, keepdims=True)
                d_all[t, r : r + 1, :] = jnp.sum(e * prob_grad[part_rows(b)], axis=0, keepdims=True)

        over_tiles(lambda group: [one(t) for t in group])

    def pass_two(where):
        def several(group):
            key_sum = value_sum = None
            for t in group:
                probs, score_grads = [], []
                for b in range(blocks):
                    r = where * blocks + b
                    prob = e_all[where, t, part_rows(b)] * factor[t, r : r + 1, :]
                    probs.append(prob.astype(BF16))
                    score_grads.append((prob * (p_all[where, t, part_rows(b)] - delta[t, 0:1, :])).astype(BF16))
                prob = jnp.concatenate(probs, axis=0)
                score_grad = jnp.concatenate(score_grads, axis=0)
                half, columns = t // heads, head_columns(t % heads)
                v = jnp.dot(prob, g_raw[half, :, columns], preferred_element_type=F32)
                k = jnp.dot(score_grad, q_raw[half, :, columns], preferred_element_type=F32)
                value_sum = v if value_sum is None else value_sum + v
                key_sum = k if key_sum is None else key_sum + k
                dq_cols[t] += jnp.dot(k_cols[where], score_grad, preferred_element_type=F32)
            term[where, VALUE] = value_sum
            term[where, KEY] = key_sum * softmax_scale

        over_tiles(several)

    for copy in own:
        copy.wait()
    spread(0)
    pair_q.wait_recv()
    pair_g.wait_recv()
    spread(1)

    def relay(distance, part):
        for b in range(blocks):
            for way in (UP, DOWN):
                if travels(way, distance, b):
                    gather_copy(way, distance, part, b).wait_recv()
                    if travels(way, distance + 1, b):
                        start(gather_copy(way, distance + 1, part, b), sends)

    work = [functools.partial(pass_one, 0, me, diagonal=True)]
    for distance in range(1, far):
        relay(distance, KEY)
        work.pop(0)()
        work.append(functools.partial(pass_one, slot(UP, distance), at_chip(-distance)))
        work.append(functools.partial(pass_one, slot(DOWN, distance), at_chip(distance)))
        relay(distance, VALUE)
        work.pop(0)()
    for item in work:
        item()
    relay(far, KEY)
    relay(far, VALUE)
    pass_one(far, at_chip(far))

    for t in range(tiles):
        visible = key_block[...] <= query_block[t // heads, 0:1, :]
        top = jnp.max(jnp.where(visible, m_all[t], HIDDEN), axis=0, keepdims=True)
        weight = jnp.where(visible, jnp.exp2((m_all[t] - top) * exponent_scale), 0.0)
        stat_out[t, 0:1, :] = top
        stat_out[t, 1:2, :] = jnp.sum(l_all[t] * weight, axis=0, keepdims=True)
        stat_out[t, 2:3, :] = jnp.sum(d_all[t] * weight, axis=0, keepdims=True)
        factor[t] = weight
    stat_copies = []
    for i in range(2):
        here, there = pl.ds(i * heads, heads), pl.ds((1 - i) * heads, heads)
        stat_copies.append(pair_copy(2 + i, stat_out.at[here], stat_in.at[there]))
        start(stat_copies[-1])
    for copy in stat_copies:
        copy.wait_recv()
    for t in range(tiles):
        top_here, top_there = stat_out[t, 0:1, :], stat_in[t, 0:1, :]
        top = jnp.maximum(top_here, top_there)
        here = jnp.exp2((top_here - top) * exponent_scale)
        there = jnp.exp2((top_there - top) * exponent_scale)
        inverse = 1.0 / (stat_out[t, 1:2, :] * here + stat_in[t, 1:2, :] * there)
        delta[t, 0:1, :] = (stat_out[t, 2:3, :] * here + stat_in[t, 2:3, :] * there) * inverse
        factor[t] = factor[t] * (here * inverse)

    def ring_step(way, distance, part, b):
        if not travels(way, distance, b):
            return
        value = term[slot(1 - way, distance), part, part_rows(b)]
        if travels(way, distance + 1, b):
            ring_copy(way, distance + 1, part, b).wait_recv()
            value = value + ring_in[way, distance, part, b].astype(F32)
        ring_out[way, distance - 1, part, b] = value.astype(BF16)
        start(ring_copy(way, distance, part, b), sends)

    def ring_steps(distance, part, first):
        for way in (UP, DOWN):
            for b in range(blocks):
                if travels(way, far, b) != first:
                    ring_step(way, distance, part, b)

    near = far - 1
    pass_two(far)
    for part in (KEY, VALUE):
        ring_steps(far, part, False)
    work = []
    for distance in range(near, 0, -1):
        for way in (UP, DOWN):
            work.append((distance, way))
    for distance, way in work[:2]:
        pass_two(slot(1 - way, distance))
        for part in (KEY, VALUE):
            for b in range(blocks):
                if not travels(way, far, b):
                    ring_step(way, distance, part, b)
    work = [functools.partial(pass_two, slot(1 - way, distance)) for distance, way in work[2:]]
    work.append(functools.partial(pass_two, 0))
    work.pop(0)()
    ring_steps(near, KEY, False)
    ring_steps(near, VALUE, False)
    for distance in range(near - 1, 0, -1):
        work.pop(0)()
        ring_steps(distance, KEY, True)
        ring_steps(distance, VALUE, True)
        if work:
            work.pop(0)()
        if distance == 1:
            for item in work:
                item()
            pair_dq = pair_copy(4, dq_cols.at[pl.ds(heads, heads)], dq_recv)
            start(pair_dq)
        ring_steps(distance, KEY, False)
        ring_steps(distance, VALUE, False)

    pair_dq.wait_recv()
    for h in range(heads):
        total = (dq_cols[h] + dq_recv[h]) * softmax_scale
        dq_stage[:, head_columns(h)] = total.T.astype(BF16)
    out = [pltpu.make_async_copy(dq_stage, dq_out, local_sem.at[5])]
    out[0].start()
    for part, stage, target in ((VALUE, dv_stage, dv_out), (KEY, dk_stage, dk_out)):
        for b in range(blocks):
            value = term[0, part, part_rows(b)]
            for way in (UP, DOWN):
                ring_copy(way, 1, part, b).wait_recv()
                value = value + ring_in[way, 0, part, b].astype(F32)
            stage[part_rows(b)] = value.astype(BF16)
        copy = pltpu.make_async_copy(stage, target, local_sem.at[6 + part])
        copy.start()
        out.append(copy)
    tile_sends = 2 * rows // half_rows * rows // head_size
    assert len(sends) % tile_sends == 0
    span = e_all.at[0, pl.ds(0, len(sends) // tile_sends)]
    pltpu.make_async_copy(span, span, sent.at[0]).wait()
    for copy in started:
        copy.wait_send()
    for copy in out:
        copy.wait()


def hand_over(*refs):
    count = len(refs) // 2
    for source, target in zip(refs[:count], refs[count:]):
        target[...] = source[...]


def solution(mesh):
    devices = mesh.shape["ctx"]
    chips = devices // 2
    far = chips // 2

    def on_device(queries, keys, values, out_grad, span_order):
        rows, head_size = keys.shape
        heads = queries.shape[1] // head_size
        tiles = 2 * heads
        spans = span_order.shape[0] // 2
        half_rows = devices * rows // span_order.shape[0]
        blocks = rows // half_rows
        any_spec = pl.BlockSpec(memory_space=pl.ANY)
        hbm_spec = pl.BlockSpec(memory_space=pltpu.HBM)
        vmem = pltpu.VMEM
        elements = chips * tiles * rows * rows
        out_shape = (
            jax.ShapeDtypeStruct(queries.shape, BF16),
            jax.ShapeDtypeStruct(keys.shape, BF16),
            jax.ShapeDtypeStruct(values.shape, BF16),
        )
        ring_semaphores = pltpu.SemaphoreType.DMA((2, far, 2, blocks))
        results = pl.pallas_call(
            functools.partial(kernel, chips, heads),
            name="ring_attention_backward",
            out_shape=out_shape,
            in_specs=[hbm_spec] * 5,
            out_specs=(any_spec,) * 3,
            scratch_shapes=[
                vmem((2, rows, heads * head_size), BF16),
                vmem((2, rows, heads * head_size), BF16),
                vmem((tiles, head_size, rows), BF16),
                vmem((tiles, head_size, rows), BF16),
                vmem((chips, rows, head_size), BF16),
                vmem((chips, rows, head_size), BF16),
                vmem((chips, head_size, rows), BF16),
                vmem((chips, tiles, rows, rows), F32),
                vmem((chips, tiles, rows, rows), F32),
                vmem((tiles, spans, rows), F32),
                vmem((tiles, spans, rows), F32),
                vmem((tiles, spans, rows), F32),
                vmem((tiles, 8, rows), F32),
                vmem((tiles, 8, rows), F32),
                vmem((tiles, spans, rows), F32),
                vmem((tiles, 8, rows), F32),
                vmem((2, 8, rows), jnp.int32),
                vmem((spans, rows), jnp.int32),
                vmem((chips, 2, rows, head_size), F32),
                vmem((tiles, head_size, rows), F32),
                vmem((heads, head_size, rows), F32),
                vmem((2, far, 2, blocks, half_rows, head_size), BF16),
                vmem((2, far, 2, blocks, half_rows, head_size), BF16),
                vmem((rows, heads * head_size), BF16),
                vmem((rows, head_size), BF16),
                vmem((rows, head_size), BF16),
                pltpu.SMEM(span_order.shape, jnp.int32),
                pltpu.SemaphoreType.DMA((8,)),
                pltpu.SemaphoreType.DMA((5,)),
                pltpu.SemaphoreType.DMA((5,)),
                pltpu.SemaphoreType.DMA((1,)),
                ring_semaphores,
                ring_semaphores,
            ],
            compiler_params=pltpu.CompilerParams(
                collective_id=0,
                has_side_effects=True,
                vmem_limit_bytes=58 * 1024 * 1024,
            ),
            cost_estimate=pl.CostEstimate(
                flops=10 * elements * head_size,
                bytes_accessed=2 * (2 * queries.size * 2 + 3 * keys.size * 2),
                transcendentals=elements,
            ),
        )(queries, keys, values, out_grad, span_order)
        return pl.pallas_call(
            hand_over,
            name="hand_over",
            out_shape=out_shape,
            in_specs=[pl.BlockSpec(memory_space=pltpu.VMEM)] * 3,
            out_specs=(pl.BlockSpec(memory_space=pltpu.VMEM),) * 3,
        )(*results)

    row = P(("dp", "ctx"), None)
    return jax.shard_map(
        on_device,
        mesh=mesh,
        in_specs=(row, row, row, row, P("dp")),
        out_specs=(row, row, row),
        check_vma=False,
    )
```
